256 devices in a mesh: node: 32 (over z, y), local: 8 (over x, core).
Axes of the slice: x: 4, y: 4, z: 8, core: 2. Of those that a mesh axis runs over, the one named last changes fastest.
Arguments:
- queries: bfloat16 [262144, 512], P(('node', 'local')), may hold values from -600 to 600
- keys: bfloat16 [262144, 128], P(('node', 'local')), may hold values from -7 to 7
- values: bfloat16 [262144, 128], P(('node', 'local')), may hold values from -6 to 6
- selected: int32 [2048, 3], P(('node', 'local')), may hold values from -1 to 511, as said below
Outputs:
- attended: bfloat16 [262144, 512], P(('node', 'local'))
The draws below stay inside these ranges and needn't reach their ends.
Inputs may be any that keep to these rules, and one draw needn't show every extreme that they name: `selected`: row t belongs to query tile t. Every entry that is not -1 names a block that lies wholly before the tile's own block, the entries of a row are distinct, and -1 entries stand only after the others. The entries of a row fall in at most two node groups (a node group is 16 consecutive blocks). Over the rows of one device, the entries that fall in one node group are at most 3 and name at most 2 distinct blocks; both bounds are reached in every draw. The entries of the rows of one device fall in at most 8 distinct node groups, or 32 if that is fewer, and some device reaches that number in every draw. Every device outside the first node group has tiles that name blocks of the first node group.
All inputs are finite; a program needn't handle non-finite values.
Results may differ from the reference program's by a relative error of at most 0.0042.
Values may be sent and summed in bfloat16 or wider, within the bound.
A program may use at most 128 MiB of HBM per device.

```python
import math
import jax
import jax.numpy as jnp
from jax import lax

HEAD_DIM = 128
HEADS = 4
TILE = 128
BLOCK = 512
TOK_DEV = 1024
NODE_COUNT = 32
GROUP_DEVS = 8
TOKENS = 262144
NUM_TILES = 2048


def base_keys(key):
    return jnp.clip(jax.random.normal(key, (TOKENS, HEAD_DIM), jnp.float32), -6.0, 6.0)


def draw_keys(key, part):
    shared = base_keys(key)
    return shared.astype(jnp.bfloat16)


def draw_queries(key, part):
    key = jax.random.fold_in(key, 7)
    fresh = jnp.clip(jax.random.normal(key, (TOKENS, HEADS * HEAD_DIM), jnp.float32), -6.0, 6.0)
    return fresh.astype(jnp.bfloat16)


def draw_selected(key, part):
    key = jax.random.fold_in(key, 11)
    device_count = NODE_COUNT * GROUP_DEVS
    tiles_dev = TOK_DEV // TILE
    blocks_dev = TOK_DEV // BLOCK
    group_blocks = GROUP_DEVS * blocks_dev
    device = jnp.arange(device_count)
    node_of = device // GROUP_DEVS
    local_of = device % GROUP_DEVS
    groups = jnp.arange(NODE_COUNT)
    earlier_group = groups[None, :] < node_of[:, None]
    own_group = (groups[None, :] == node_of[:, None]) & (local_of[:, None] * blocks_dev >= 3)
    candidate = earlier_group | own_group
    limit = jnp.where(earlier_group, group_blocks, local_of[:, None] * blocks_dev)
    key_perm, key_first, key_second = jax.random.split(key, 3)
    perm_keys = jax.random.split(key_perm, device_count)
    ranking = jax.vmap(lambda k: jax.random.permutation(k, NODE_COUNT))(perm_keys)
    ranking = jnp.where(candidate, ranking, ranking + NODE_COUNT)
    ranking = jnp.where((groups[None, :] == 0) & earlier_group, -1, ranking)
    order = jnp.argsort(ranking, axis=1, stable=True)
    taken = min(tiles_dev, NODE_COUNT)
    picks = order[:, :taken]
    usable = jnp.take_along_axis(candidate, picks, axis=1)
    lim = jnp.take_along_axis(limit, picks, axis=1)
    if tiles_dev > NODE_COUNT:
        extra = tiles_dev - NODE_COUNT
        picks = jnp.concatenate([picks, jnp.zeros((device_count, extra), picks.dtype)], axis=1)
        usable = jnp.concatenate([usable, jnp.zeros((device_count, extra), bool)], axis=1)
        lim = jnp.concatenate([lim, jnp.full((device_count, extra), 3, lim.dtype)], axis=1)
    lim = jnp.where(usable, lim, 3)
    first_raw = jax.random.randint(key_first, (device_count, tiles_dev), 0, 1 << 20) % (lim - 1)
    step_raw = 1 + jax.random.randint(key_second, (device_count, tiles_dev), 0, 1 << 20) % (lim - 2)
    first_off = 1 + first_raw
    second_off = 1 + (first_raw + step_raw) % (lim - 1)
    first_id = jnp.where(usable, picks * group_blocks + first_off, -1)
    second_id = jnp.where(usable, picks * group_blocks + second_off, -1)
    a_one = first_id[:, 0::2]
    a_two = second_id[:, 0::2]
    b_one = first_id[:, 1::2]
    b_two = second_id[:, 1::2]
    tile_a = jnp.stack([a_one, a_two, b_one], axis=-1)
    tile_b = jnp.stack([a_one, b_one, b_two], axis=-1)
    rows = jnp.stack([tile_a, tile_b], axis=2)
    return rows.reshape(device_count * tiles_dev, 3).astype(jnp.int32)


def shard_levels(rng, extent, shards, smallest, largest):
    gain = 1.0
    for position, parts in shards:
        heights = jax.random.uniform(jax.random.fold_in(jax.random.fold_in(rng, 6), position), (parts,), jnp.float32, smallest / len(shards), largest / len(shards))
        gain = gain * jnp.repeat(jnp.exp(heights), extent[position] // parts).reshape((-1,) + (1,) * (len(extent) - 1 - position))
    return gain


def scatter_about(stream_key, dims, scale, most, cuts=(), held_as=jnp.bfloat16):
    entries = jax.random.normal(stream_key, dims, jnp.float32) * scale
    if len(cuts) > 0:
        entries = shard_levels(stream_key, dims, cuts, -0.22, 0.18) * entries
    return jnp.clip(entries, min=-most, max=most).astype(held_as)


def setup_inputs(seed: int = 0) -> dict:
    arg_keys = jax.random.split(jax.random.key(seed), 5)
    queries = draw_queries(jax.random.fold_in(arg_keys[4], 71), 0)
    keys = draw_keys(jax.random.fold_in(arg_keys[4], 71), 0)
    values = scatter_about(arg_keys[2], (TOKENS, HEAD_DIM), 1.0, 6.0, ((0, 256),))
    selected = draw_selected(jax.random.fold_in(arg_keys[4], 71), 0)
    return {"queries": queries, "keys": keys, "values": values, "selected": selected}


def reference(queries, keys, values, selected):
    score_scale = 1.0 / math.sqrt(HEAD_DIM)

    def attend(tile_index):
        first_row = (tile_index * TILE).astype(jnp.int32)
        tile_q = lax.dynamic_slice_in_dim(queries, first_row, TILE, 0).astype(jnp.float32)
        tile_q = tile_q.reshape(TILE, HEADS, HEAD_DIM)
        chosen_ids = lax.dynamic_index_in_dim(selected, tile_index, 0, keepdims=False)
        key_parts = []
        value_parts = []
        live_parts = []
        for entry in range(3):
            block_id = jnp.maximum(chosen_ids[entry], 0).astype(jnp.int32)
            block_row = (block_id * BLOCK).astype(jnp.int32)
            key_parts.append(lax.dynamic_slice_in_dim(keys, block_row, BLOCK, 0))
            value_parts.append(lax.dynamic_slice_in_dim(values, block_row, BLOCK, 0))
            live_parts.append(jnp.broadcast_to(chosen_ids[entry] >= 0, (TILE, BLOCK)))
        block_start = (first_row // BLOCK * BLOCK).astype(jnp.int32)
        key_parts.append(lax.dynamic_slice_in_dim(keys, block_start, BLOCK, 0))
        value_parts.append(lax.dynamic_slice_in_dim(values, block_start, BLOCK, 0))
        key_pos = block_start + jnp.arange(BLOCK, dtype=jnp.int32)
        query_pos = first_row + jnp.arange(TILE, dtype=jnp.int32)
        live_parts.append(key_pos[None, :] <= query_pos[:, None])
        all_keys = jnp.concatenate(key_parts, axis=0).astype(jnp.float32)
        all_values = jnp.concatenate(value_parts, axis=0).astype(jnp.float32)
        allowed = jnp.concatenate(live_parts, axis=1)
        scores = jnp.einsum('qhd,kd->hqk', tile_q, all_keys) * score_scale
        scores = jnp.where(allowed[None, :, :], scores, -jnp.inf)
        row_max = lax.optimization_barrier(jnp.max(scores, axis=2, keepdims=True))
        weights = jnp.exp(scores - row_max)
        row_sum = lax.optimization_barrier(jnp.sum(weights, axis=2))
        rounded = lax.optimization_barrier(weights.astype(jnp.bfloat16)).astype(jnp.float32)
        weighted = jnp.einsum('hqk,kd->qhd', rounded, all_values)
        normed = weighted / jnp.transpose(row_sum)[:, :, None]
        return normed.reshape(TILE, HEADS * HEAD_DIM).astype(jnp.bfloat16)
    tiles_out = lax.map(attend, jnp.arange(NUM_TILES, dtype=jnp.int32))
    return tiles_out.reshape(TOKENS, HEADS * HEAD_DIM)
```

```python
import functools
import math

import jax
import jax.numpy as jnp
from jax import lax
from jax.experimental import pallas as pl
from jax.experimental.pallas import tpu as pltpu
from jax.sharding import PartitionSpec as P

MESH = pl.DeviceIdType.MESH
BF16 = jnp.bfloat16
F32 = jnp.float32

TILE = 128
BLOCK = 512
HEADS = 4
DIM = 128
NX, NY, NZ = 4, 4, 8
CHIPS = NX * NY
SLOTS = 16
ENTRIES = 24
TILES = 8
UNIT = CHIPS * 2
STORE = NZ * 2 * UNIT
UP_STEPS, DOWN_STEPS = 4, 3
LAST_DOWN = 2
SCALE2 = math.log2(math.e) / math.sqrt(DIM)
DEAD = -1e30

ORDER = [
    (0, 1), (0, 3), (1, 0), (3, 0), (1, 1), (3, 3), (1, 3), (3, 1),
    (0, 2), (2, 0), (2, 2), (1, 2), (3, 2), (2, 1), (2, 3),
]


def device(z, y, x, c):
    return (z * NY + y, x * 2 + c)


def kernel(
    q_ref, k_ref, v_ref, slots_ref, emap_ref, out_ref,
    st0, st1, st2, st3, sb0, sb1, sb2, sb3, rb0, rb1, rb2, rb3,
    req, idxv, idxs, p_ref, m_ref, l_ref, acc_ref,
    rq_send, rq_recv, ix_sem, t_send, t_recv, z_send, z_recv, s_send, s_recv, g_send, g_recv,
):
    store = [st0, st1, st2, st3]
    outgoing = [sb0, sb1, sb2, sb3]
    arrived = [rb0, rb1, rb2, rb3]
    node = lax.axis_index("node")
    local = lax.axis_index("local")
    z, y, x, c = node // NY, node % NY, local // 2, local % 2
    chip = y * NX + x

    def partner(dy, dx):
        return device(z, (y + dy) % NY, (x + dx) % NX, c)

    above = device((z + 1) % NZ, y, x, c)
    below = device((z + NZ - 1) % NZ, y, x, c)
    sibling = device(z, y, x, 1 - c)

    barrier = pltpu.get_barrier_semaphore()
    for dy, dx in ORDER:
        pl.semaphore_signal(barrier, inc=1, device_id=partner(dy, dx), device_id_type=MESH)
    for other in (above, below, sibling):
        pl.semaphore_signal(barrier, inc=1, device_id=other, device_id_type=MESH)
    pl.semaphore_wait(barrier, len(ORDER) + 3)

    for dy, dx in ORDER:
        pltpu.make_async_remote_copy(
            slots_ref, req.at[dy * NX + dx], rq_send, rq_recv,
            device_id=partner(dy, dx), device_id_type=MESH,
        ).start()
    req[0] = slots_ref[...]

    def source(q, piece):
        ref = k_ref if q < 2 else v_ref
        return ref.at[:, piece, q % 2]

    def unit(q, plane, core):
        return store[q].at[pl.ds((plane * 2 + core) * UNIT, UNIT)]

    for q in range(4):
        for dy, dx in ORDER:
            to = ((y + dy) % NY) * NX + (x + dx) % NX
            offset = dy * NX + dx
            pltpu.make_async_remote_copy(
                source(q, to),
                store[q].at[pl.ds((z * 2 + c) * UNIT + offset * 2, 2)],
                t_send.at[q], t_recv.at[q],
                device_id=partner(dy, dx), device_id_type=MESH,
            ).start()
        store[q][pl.ds((z * 2 + c) * UNIT, 2)] = source(q, chip)[...]

    def spread_wait(q):
        rest = store[q].at[pl.ds((z * 2 + c) * UNIT + 2, UNIT - 2)]
        pltpu.make_async_copy(rest, rest, t_recv.at[q]).wait()

    pltpu.make_async_copy(req.at[pl.ds(1, CHIPS - 1)], req.at[pl.ds(1, CHIPS - 1)], rq_recv).wait()
    ids = req[:, 0, :]
    offset_y = (y + NY - (ids // 16) % NY) % NY
    offset_x = (x + NX - (ids // 4) % NX) % NX
    idxv[...] = (ids // 64 * 2 + (ids // 2) % 2) * UNIT + (offset_y * NX + offset_x) * 2 + ids % 2
    fetch = pltpu.make_async_copy(idxv, idxs, ix_sem)
    fetch.start()
    fetch.wait()

    def up_copy(q, t):
        piece = unit(q, z - t, c)
        return pltpu.make_async_remote_copy(
            piece, piece, z_send.at[q, 0, t], z_recv.at[q, 0, t],
            device_id=above, device_id_type=MESH,
        )

    def down_copy(q, t):
        piece = unit(q, (z + t) % NZ, c)
        return pltpu.make_async_remote_copy(
            piece, piece, z_send.at[q, 1, t], z_recv.at[q, 1, t],
            device_id=below, device_id_type=MESH,
        )

    def across_copy(q, plane):
        piece = unit(q, plane, c)
        return pltpu.make_async_remote_copy(
            piece, piece, s_send.at[q, plane], s_recv.at[q, plane],
            device_id=sibling, device_id_type=MESH,
        )

    def sends_up(t):
        return (z - t >= 0) & (z < NZ - 1)

    def sends_down(t):
        return (z + t) % NZ <= LAST_DOWN

    def gets_up(t):
        return z - 1 - t >= 0

    def gets_down(t):
        return (z + 1 + t) % NZ <= LAST_DOWN

    def ring_step(q, t):
        if t == 0:
            spread_wait(q)
        if 1 <= t <= UP_STEPS:
            @pl.when(gets_up(t - 1))
            def _():
                piece = unit(q, z - t, c)
                pltpu.make_async_copy(piece, piece, z_recv.at[q, 0, t - 1]).wait()
        if t < UP_STEPS:
            @pl.when(sends_up(t))
            def _():
                up_copy(q, t).start()
        if 1 <= t <= DOWN_STEPS:
            @pl.when(gets_down(t - 1))
            def _():
                piece = unit(q, (z + t) % NZ, c)
                pltpu.make_async_copy(piece, piece, z_recv.at[q, 1, t - 1]).wait()
        if t < DOWN_STEPS:
            @pl.when(sends_down(t))
            def _():
                down_copy(q, t).start()
        if t == 0:
            across_copy(q, z).start()
        else:
            if t <= UP_STEPS:
                @pl.when(gets_up(t - 1))
                def _():
                    across_copy(q, z - t).start()
            if t <= DOWN_STEPS:
                @pl.when(gets_down(t - 1) & ((z + t) % NZ < z))
                def _():
                    across_copy(q, (z + t) % NZ).start()

    def across_wait(q):
        for plane in range(NZ):
            @pl.when(plane <= z)
            def _():
                piece = unit(q, plane, 1 - c)
                pltpu.make_async_copy(piece, piece, s_recv.at[q, plane]).wait()

    def ring_drain(q):
        for t in range(UP_STEPS):
            @pl.when(sends_up(t))
            def _():
                up_copy(q, t).wait_send()
        for t in range(DOWN_STEPS):
            @pl.when(sends_down(t))
            def _():
                down_copy(q, t).wait_send()
        for plane in range(NZ):
            @pl.when(plane <= z)
            def _():
                across_copy(q, plane).wait_send()

    def gather(q):
        def fill(offset, carry):
            asked = ((NY - offset // NX) % NY) * NX + (NX - offset % NX) % NX
            for s in range(SLOTS):
                outgoing[q][offset, s] = store[q][idxs[asked, s]]
            return carry

        lax.fori_loop(1, CHIPS, fill, 0)
        for s in range(SLOTS):
            arrived[q][0, s] = store[q][idxs[0, s]]
        for dy, dx in ORDER:
            offset = dy * NX + dx
            pltpu.make_async_remote_copy(
                outgoing[q].at[offset], arrived[q].at[offset], g_send.at[q], g_recv.at[q],
                device_id=partner(dy, dx), device_id_type=MESH,
            ).start()

    def gather_wait(q):
        rest = arrived[q].at[pl.ds(1, CHIPS - 1)]
        pltpu.make_async_copy(rest, rest, g_recv.at[q]).wait()

    def stacked(t):
        rows = pl.ds(t * TILE, TILE)
        return jnp.concatenate([q_ref[rows, h * DIM:(h + 1) * DIM] for h in range(HEADS)], axis=0)

    def scores(a, b):
        return lax.dot_general(a, b, (((1,), (1,)), ((), ())), preferred_element_type=F32)

    def own(block, carry):
        for r in range(BLOCK // TILE):
            t = block * (BLOCK // TILE) + r
            width = (r + 1) * TILE
            keys = k_ref[block].reshape(BLOCK, DIM)[:width]
            vals = v_ref[block].reshape(BLOCK, DIM)[:width]
            s = scores(stacked(t), keys)
            row = lax.broadcasted_iota(jnp.int32, s.shape, 0) % TILE + r * TILE
            col = lax.broadcasted_iota(jnp.int32, s.shape, 1)
            s = jnp.where(col <= row, s, -jnp.inf)
            m = jnp.max(s, axis=1, keepdims=True)
            p = jnp.exp2(s * SCALE2 - m * SCALE2)
            m_ref[t] = m
            l_ref[t] = jnp.sum(p, axis=1, keepdims=True)
            acc_ref[t] = jnp.dot(p.astype(BF16), vals, preferred_element_type=F32)
        return carry

    def slot_of(t, e):
        entry = emap_ref[t * 3 + e]
        return jnp.maximum(entry, 0), jnp.where(entry < 0, DEAD, 0.0).astype(F32)

    def remote_keys(t, carry):
        queries = stacked(t)
        m_own = m_ref[t]
        m = m_own
        parts = []
        for e in range(3):
            slot, bias = slot_of(t, e)
            keys = jnp.concatenate(
                [rb0[:, slot].reshape(BLOCK // 2, DIM), rb1[:, slot].reshape(BLOCK // 2, DIM)], axis=0)
            s = scores(queries, keys)
            m = jnp.maximum(m, jnp.max(s, axis=1, keepdims=True) + bias)
            parts.append((s, bias))
        m2 = m * SCALE2
        alpha = jnp.exp2(m_own * SCALE2 - m2)
        total = l_ref[t] * alpha
        for e, (s, bias) in enumerate(parts):
            p = jnp.exp2(s * SCALE2 - (m2 - bias))
            total = total + jnp.sum(p, axis=1, keepdims=True)
            p_ref[t * 3 + e] = p.astype(BF16)
        l_ref[t] = total
        acc_ref[t] = acc_ref[t] * alpha
        return carry

    def remote_values(half, last):
        ref = arrived[2 + half]

        def step(t, carry):
            acc = acc_ref[t]
            for e in range(3):
                slot, _ = slot_of(t, e)
                vals = ref[:, slot].reshape(BLOCK // 2, DIM)
                p = p_ref[t * 3 + e, :, half * (BLOCK // 2):(half + 1) * (BLOCK // 2)]
                acc = acc + jnp.dot(p, vals, preferred_element_type=F32)
            if last:
                normed = (acc / l_ref[t]).astype(BF16)
                for h in range(HEADS):
                    out_ref[pl.ds(t * TILE, TILE), h * DIM:(h + 1) * DIM] = normed[h * TILE:(h + 1) * TILE]
            else:
                acc_ref[t] = acc
            return carry

        lax.fori_loop(0, TILES, step, 0)

    for q in range(4):
        for t in range(UP_STEPS + 1):
            ring_step(q, t)
        if q == 0:
            lax.fori_loop(0, 2, own, 0)
        across_wait(q)
        gather(q)
    gather_wait(0)
    gather_wait(1)
    lax.fori_loop(0, TILES, remote_keys, 0)
    gather_wait(2)
    remote_values(0, False)
    gather_wait(3)
    remote_values(1, True)

    pltpu.make_async_copy(req.at[pl.ds(1, CHIPS - 1)], req.at[pl.ds(1, CHIPS - 1)], rq_send).wait()
    for q in range(4):
        rest = store[q].at[pl.ds(0, UNIT - 2)]
        pltpu.make_async_copy(rest, rest, t_send.at[q]).wait()
        ring_drain(q)
        rest = outgoing[q].at[pl.ds(1, CHIPS - 1)]
        pltpu.make_async_copy(rest, rest, g_send.at[q]).wait()


def plan_slots(selected, first_block):
    entries = selected.reshape(-1)
    count = entries.shape[0]
    position = jnp.arange(count)
    usable = entries >= 0
    same = (entries[:, None] == entries[None, :]) & usable[:, None]
    first = usable & ~jnp.any(same & (position[None, :] < position[:, None]), axis=1)
    rank = jnp.sum((first[None, :] & (position[None, :] < position[:, None])).astype(jnp.int32), axis=1)
    slot = jnp.sum(jnp.where(same & first[None, :], rank[None, :], 0), axis=1)
    slot = jnp.where(usable, slot, -1)
    lanes = jnp.arange(128)
    hit = first[:, None] & (rank[:, None] == lanes[None, :])
    ids = jnp.where(jnp.any(hit, axis=0), jnp.sum(jnp.where(hit, entries[:, None], 0), axis=0), first_block)
    return jnp.broadcast_to(ids[None, :], (8, 128)).astype(jnp.int32), slot.astype(jnp.int32)


def body(queries, keys, values, selected):
    tokens = keys.shape[0]
    plane = lax.axis_index("node") // NY
    slots, emap = plan_slots(selected, plane * (CHIPS * 4))
    view = (tokens // BLOCK, CHIPS, 2, 16, DIM)
    vmem = pl.BlockSpec(memory_space=pltpu.VMEM)
    smem = pl.BlockSpec(memory_space=pltpu.SMEM)
    dma = pltpu.SemaphoreType.DMA
    scratch = (
        [pltpu.VMEM((STORE, 16, DIM), BF16)] * 4
        + [pltpu.VMEM((CHIPS, SLOTS, 16, DIM), BF16)] * 8
        + [
            pltpu.VMEM((CHIPS, 8, 128), jnp.int32),
            pltpu.VMEM((CHIPS, 128), jnp.int32),
            pltpu.SMEM((CHIPS, 128), jnp.int32),
            pltpu.VMEM((TILES * 3, HEADS * TILE, BLOCK), BF16),
            pltpu.VMEM((TILES, HEADS * TILE, 1), F32),
            pltpu.VMEM((TILES, HEADS * TILE, 1), F32),
            pltpu.VMEM((TILES, HEADS * TILE, DIM), F32),
            dma, dma, dma,
            dma((4,)), dma((4,)),
            dma((4, 2, UP_STEPS)), dma((4, 2, UP_STEPS)),
            dma((4, NZ)), dma((4, NZ)),
            dma((4,)), dma((4,)),
        ]
    )
    return pl.pallas_call(
        kernel,
        out_shape=jax.ShapeDtypeStruct(queries.shape, BF16),
        in_specs=[vmem, vmem, vmem, vmem, smem],
        out_specs=vmem,
        scratch_shapes=scratch,
        compiler_params=pltpu.CompilerParams(
            collective_id=0, has_side_effects=True, vmem_limit_bytes=56 << 20),
        cost_estimate=pl.CostEstimate(flops=4 << 30, bytes_accessed=8 << 20, transcendentals=8 << 20),
        name="moba",
    )(queries, keys.reshape(view), values.reshape(view), slots, emap)


def solution(mesh):
    spec = P(("node", "local"), None)
    return jax.shard_map(
        body, mesh=mesh, in_specs=(spec,) * 4, out_specs=spec, check_vma=False)
```

```python
import functools
import math

import jax
import jax.numpy as jnp
from jax import lax
from jax.experimental import pallas as pl
from jax.experimental.pallas import tpu as pltpu
from jax.sharding import PartitionSpec as P

MESH = pl.DeviceIdType.MESH
BF16 = jnp.bfloat16
F32 = jnp.float32

TILE = 128
BLOCK = 512
KHALF = BLOCK // 2
HEADS = 4
DIM = 128
NX, NY, NZ = 4, 4, 8
CHIPS = NX * NY
SLOTS = 16
ENTRIES = 24
TILES = 8
UNIT = CHIPS * 2
STORE = NZ * 2 * UNIT
PIECES = 4
PIECE = UNIT // PIECES
UP_STEPS, DOWN_STEPS = (4, 3) * (PIECES // 2), (3, 4) * (PIECES // 2)
OWN_EVERY = 0.5
AHEAD = 0.3
RING_STEPS = 4
SCALE2 = math.log2(math.e) / math.sqrt(DIM)
DEAD = -1e30

ORDER = [
    (0, 1), (0, 3), (1, 0), (3, 0), (1, 1), (3, 3), (1, 3), (3, 1),
    (0, 2), (2, 0), (2, 2), (1, 2), (3, 2), (2, 1), (2, 3),
]


def device(z, y, x, c):
    return (z * NY + y, x * 2 + c)


def kernel(
    q_hbm, k_hbm, v_hbm, sel_hbm, out_hbm,
    q_ref, k_ref, v_ref, sel_ref, out_ref,
    st0, st1, st2, st3, sb0, sb1, sb2, sb3, rb0, rb1, rb2, rb3,
    emap, wanted, req, idxv, idxs, p_ref, m_ref, l_ref, acc_ref,
    in_sem, out_sem, rq_send, rq_recv, ix_sem, t_send, t_recv, z_send, z_recv, s_recv, g_send, g_recv,
):
    store = [st0, st1, st2, st3]
    outgoing = [sb0, sb1, sb2, sb3]
    arrived = [rb0, rb1, rb2, rb3]
    node = lax.axis_index("node")
    local = lax.axis_index("local")
    z, y, x, c = node // NY, node % NY, local // 2, local % 2
    chip = y * NX + x

    def partner(dy, dx):
        return device(z, (y + dy) % NY, (x + dx) % NX, c)

    above = device((z + 1) % NZ, y, x, c)
    below = device((z + NZ - 1) % NZ, y, x, c)
    sibling = device(z, y, x, 1 - c)

    loads = [
        pltpu.make_async_copy(src, dst, in_sem.at[i])
        for i, (src, dst) in enumerate(
            [(sel_hbm, sel_ref), (k_hbm, k_ref), (v_hbm, v_ref), (q_hbm, q_ref)])
    ]
    barrier = pltpu.get_barrier_semaphore()
    for dy, dx in ORDER:
        pl.semaphore_signal(barrier, inc=1, device_id=partner(dy, dx), device_id_type=MESH)
    for other in (above, below, sibling):
        pl.semaphore_signal(barrier, inc=1, device_id=other, device_id_type=MESH)

    for load in loads:
        load.start()

    loads[0].wait()
    entries = [sel_ref[j % 3, j // 3] for j in range(ENTRIES)]
    lane = lax.broadcasted_iota(jnp.int32, (8, 128), 1)
    ids = jnp.full((8, 128), z * (CHIPS * 4), jnp.int32)
    numbers = []
    count = jnp.int32(0)
    for j, entry in enumerate(entries):
        number, seen = count, entry < 0
        for i in range(j):
            same = entries[i] == entry
            number = jnp.where(same, numbers[i], number)
            seen = seen | same
        number = jnp.where(entry < 0, -1, number)
        count = jnp.where(seen, count, count + 1)
        numbers.append(number)
        emap[j] = number
        ids = jnp.where(lane == number, entry, ids)
    wanted[...] = ids

    loads[1].wait()
    pl.semaphore_wait(barrier, len(ORDER) + 3)

    def source(q, piece):
        ref = k_ref if q < 2 else v_ref
        return ref.at[:, piece, q % 2]

    def spread(q):
        for dy, dx in ORDER:
            to = ((y + dy) % NY) * NX + (x + dx) % NX
            offset = dy * NX + dx
            pltpu.make_async_remote_copy(
                source(q, to),
                store[q].at[pl.ds((c * NZ + z) * UNIT + offset * 2, 2)],
                t_send.at[q], t_recv.at[q, dy],
                device_id=partner(dy, dx), device_id_type=MESH,
            ).start()
        store[q][pl.ds((c * NZ + z) * UNIT, 2)] = source(q, chip)[...]

    def spread_wait(q, h):
        first = 2 if h == 0 else 0
        rest = store[q].at[pl.ds((c * NZ + z) * UNIT + h * PIECE + first, PIECE - first)]
        pltpu.make_async_copy(rest, rest, t_recv.at[q, h]).wait()

    def ask():
        for dy, dx in ORDER:
            pltpu.make_async_remote_copy(
                wanted, req.at[dy * NX + dx], rq_send, rq_recv,
                device_id=partner(dy, dx), device_id_type=MESH,
            ).start()
        req[0] = wanted[...]

    def places():
        rest = req.at[pl.ds(1, CHIPS - 1)]
        pltpu.make_async_copy(rest, rest, rq_recv).wait()
        ids = req[:, 0, :]
        offset_y = (y + NY - (ids // 16) % NY) % NY
        offset_x = (x + NX - (ids // 4) % NX) % NX
        idxv[...] = ((ids // 2) % 2 * NZ + ids // 64) * UNIT + (offset_y * NX + offset_x) * 2 + ids % 2
        pltpu.make_async_copy(idxv, idxs, ix_sem).start()

    def places_wait():
        pltpu.make_async_copy(idxv, idxs, ix_sem).wait()

    def piece(q, plane, core, h):
        return store[q].at[pl.ds((core * NZ + plane) * UNIT + h * PIECE, PIECE)]

    def up_copy(q, t, h):
        ref = piece(q, z - t, c, h)
        return pltpu.make_async_remote_copy(
            ref, ref, z_send.at[q], z_recv.at[q, 0, t, h],
            device_id=above, device_id_type=MESH,
        )

    def down_copy(q, t, h):
        ref = piece(q, (z + t) % NZ, c, h)
        return pltpu.make_async_remote_copy(
            ref, ref, z_send.at[q], z_recv.at[q, 1, t, h],
            device_id=below, device_id_type=MESH,
        )

    def across_copy(q, plane, h):
        ref = piece(q, plane, c, h)
        return pltpu.make_async_remote_copy(
            ref, ref, z_send.at[q], s_recv.at[q],
            device_id=sibling, device_id_type=MESH,
        )

    def sends_up(t):
        return (z - t >= 0) & (z < NZ - 1)

    def sends_down(t, h):
        return (z + t) % NZ < DOWN_STEPS[h]

    def gets_up(t):
        return z - 1 - t >= 0

    def gets_down(t, h):
        return (z + 1 + t) % NZ < DOWN_STEPS[h]

    def ring_step(q, t, h):
        if t == 0:
            spread_wait(q, h)
        if 1 <= t <= UP_STEPS[h]:
            @pl.when(gets_up(t - 1))
            def _():
                ref = piece(q, z - t, c, h)
                pltpu.make_async_copy(ref, ref, z_recv.at[q, 0, t - 1, h]).wait()
        if t < UP_STEPS[h]:
            @pl.when(sends_up(t))
            def _():
                up_copy(q, t, h).start()
        if 1 <= t <= DOWN_STEPS[h]:
            @pl.when(gets_down(t - 1, h))
            def _():
                ref = piece(q, (z + t) % NZ, c, h)
                pltpu.make_async_copy(ref, ref, z_recv.at[q, 1, t - 1, h]).wait()
        if t < DOWN_STEPS[h]:
            @pl.when(sends_down(t, h))
            def _():
                down_copy(q, t, h).start()
        if t == 0:
            across_copy(q, z, h).start()
        else:
            if t <= UP_STEPS[h]:
                @pl.when(gets_up(t - 1))
                def _():
                    across_copy(q, z - t, h).start()
            if t <= DOWN_STEPS[h]:
                @pl.when(gets_down(t - 1, h) & ((z + t) % NZ < z))
                def _():
                    across_copy(q, (z + t) % NZ, h).start()

    def across_wait(q):
        for plane in range(NZ):
            @pl.when(z == plane)
            def _():
                ref = store[q].at[pl.ds((1 - c) * NZ * UNIT, (plane + 1) * UNIT)]
                pltpu.make_async_copy(ref, ref, s_recv.at[q]).wait()

    def ring_drain(q):
        for plane in range(NZ):
            count = 0
            for h in range(PIECES):
                if plane < NZ - 1:
                    count += sum(plane - t >= 0 for t in range(UP_STEPS[h]))
                count += sum((plane + t) % NZ < DOWN_STEPS[h] for t in range(DOWN_STEPS[h]))
            tiles = count * PIECE + (plane + 1) * UNIT

            @pl.when(z == plane)
            def _():
                ref = store[q].at[pl.ds(0, tiles)]
                pltpu.make_async_copy(ref, ref, z_send.at[q]).wait()
        rest = store[q].at[pl.ds(0, UNIT - 2)]
        pltpu.make_async_copy(rest, rest, t_send.at[q]).wait()

    def gather(q, part):
        def fill(offset, carry):
            asked = ((NY - offset // NX) % NY) * NX + (NX - offset % NX) % NX
            for s in range(SLOTS):
                outgoing[q][offset, s] = store[q][idxs[asked, s]]
            return carry

        if part == 0:
            for s in range(SLOTS):
                arrived[q][0, s] = store[q][idxs[0, s]]
        for dy, dx in ORDER[part * 4:part * 4 + 4]:
            offset = dy * NX + dx
            fill(offset, 0)
            pltpu.make_async_remote_copy(
                outgoing[q].at[offset], arrived[q].at[offset], g_send.at[q], g_recv.at[q],
                device_id=partner(dy, dx), device_id_type=MESH,
            ).start()

    def gather_wait(q):
        rest = arrived[q].at[pl.ds(1, CHIPS - 1)]
        pltpu.make_async_copy(rest, rest, g_recv.at[q]).wait()

    def stacked(t):
        rows = pl.ds(t * TILE, TILE)
        return jnp.concatenate([q_ref[rows, h * DIM:(h + 1) * DIM] for h in range(HEADS)], axis=0)

    def scores(a, b):
        return lax.dot_general(a, b, (((1,), (1,)), ((), ())), preferred_element_type=F32)

    def own(t):
        block, r = t // (BLOCK // TILE), t % (BLOCK // TILE)
        width = (r + 1) * TILE
        keys = k_ref[block].reshape(BLOCK, DIM)[:width]
        vals = v_ref[block].reshape(BLOCK, DIM)[:width]
        s = scores(stacked(t), keys)
        row = lax.broadcasted_iota(jnp.int32, s.shape, 0) % TILE + r * TILE
        col = lax.broadcasted_iota(jnp.int32, s.shape, 1)
        s = jnp.where(col <= row, s, -jnp.inf)
        m = jnp.max(s, axis=1, keepdims=True)
        p = jnp.exp2(s * SCALE2 - m * SCALE2)
        m_ref[t] = m
        l_ref[t] = jnp.sum(p, axis=1, keepdims=True)
        acc_ref[t] = jnp.dot(p.astype(BF16), vals, preferred_element_type=F32)

    def slot_of(t, e):
        entry = emap[t * 3 + e]
        return jnp.maximum(entry, 0), jnp.where(entry < 0, DEAD, 0.0).astype(F32)

    def remote_keys(t, carry):
        queries = stacked(t)
        m_own = m_ref[t]
        m = m_own
        parts = []
        for e in range(3):
            slot, bias = slot_of(t, e)
            keys = jnp.concatenate(
                [rb0[:, slot].reshape(KHALF, DIM), rb1[:, slot].reshape(KHALF, DIM)], axis=0)
            s = scores(queries, keys)
            m = jnp.maximum(m, jnp.max(s, axis=1, keepdims=True) + bias)
            parts.append((s, bias))
        m2 = m * SCALE2
        alpha = jnp.exp2(m_own * SCALE2 - m2)
        total = l_ref[t] * alpha
        for e, (s, bias) in enumerate(parts):
            p = jnp.exp2(s * SCALE2 - (m2 - bias))
            total = total + jnp.sum(p, axis=1, keepdims=True)
            p = p.astype(BF16)
            for half in range(2):
                p_ref[half, t, :, e * KHALF:(e + 1) * KHALF] = p[:, half * KHALF:(half + 1) * KHALF]
        l_ref[t] = 1.0 / total
        acc_ref[t] = acc_ref[t] * alpha
        return carry

    def out_copy(rows):
        return pltpu.make_async_copy(out_ref.at[rows], out_hbm.at[rows], out_sem)

    def remote_values(half, last):
        ref = arrived[2 + half]

        def step(t, carry):
            slots = [slot_of(t, e)[0] for e in range(3)]
            vals = jnp.concatenate([ref[:, slot].reshape(KHALF, DIM) for slot in slots], axis=0)
            acc = acc_ref[t] + jnp.dot(p_ref[half, t], vals, preferred_element_type=F32)
            if last:
                normed = (acc * l_ref[t]).astype(out_ref.dtype)
                rows = pl.ds(pl.multiple_of(t * TILE, TILE), TILE)
                for h in range(HEADS):
                    out_ref[rows, h * DIM:(h + 1) * DIM] = normed[h * TILE:(h + 1) * TILE]
                out_copy(rows).start()
            else:
                acc_ref[t] = acc
            return carry

        lax.fori_loop(0, TILES, step, 0)

    spread(0)
    ask()
    spread(1)
    for h in range(PIECES):
        ring_step(0, 0, h)
    loads[2].wait()
    spread(2)
    spread(3)
    loads[3].wait()

    events = []
    for q in range(4):
        begin = 3.5 * q
        for h in range(PIECES):
            if q > 0:
                events.append((begin - AHEAD + h / PIECES, functools.partial(ring_step, q, 0, h)))
            for t in range(1, RING_STEPS + 1):
                events.append((begin + t + h / PIECES, functools.partial(ring_step, q, t, h)))
        events.append((begin + 4.8, functools.partial(across_wait, q)))
        for part in range(4):
            events.append((begin + 4.81 + 0.5 * part * (q < 3), functools.partial(gather, q, part)))
    for t in range(TILES):
        events.append((0.9 + OWN_EVERY * t, functools.partial(own, t)))
    events.append((2.1, places))
    events.append((2.9, places_wait))
    for _, task in sorted(events, key=lambda event: event[0]):
        task()

    gather_wait(0)
    gather_wait(1)
    lax.fori_loop(0, TILES, remote_keys, 0)
    rest = req.at[pl.ds(1, CHIPS - 1)]
    pltpu.make_async_copy(rest, rest, rq_send).wait()
    for q in range(4):
        ring_drain(q)
        if q < 3:
            rest = outgoing[q].at[pl.ds(1, CHIPS - 1)]
            pltpu.make_async_copy(rest, rest, g_send.at[q]).wait()
    gather_wait(2)
    remote_values(0, False)
    gather_wait(3)
    remote_values(1, True)

    out_copy(pl.ds(0, TILES * TILE)).wait()
    rest = outgoing[3].at[pl.ds(1, CHIPS - 1)]
    pltpu.make_async_copy(rest, rest, g_send.at[3]).wait()


def body(queries, keys, values, selected):
    tokens = keys.shape[0]
    view = (tokens // BLOCK, CHIPS, 2, 16, DIM)
    hbm = pl.BlockSpec(memory_space=pl.ANY)
    dma = pltpu.SemaphoreType.DMA
    scratch = (
        [
            pltpu.VMEM(queries.shape, BF16),
            pltpu.VMEM(view, BF16),
            pltpu.VMEM(view, BF16),
            pltpu.SMEM(selected.shape[::-1], jnp.int32),
            pltpu.VMEM(queries.shape, BF16),
        ]
        + [pltpu.VMEM((STORE, 16, DIM), BF16)] * 4
        + [pltpu.VMEM((CHIPS, SLOTS, 16, DIM), BF16)] * 8
        + [
            pltpu.SMEM((ENTRIES,), jnp.int32),
            pltpu.VMEM((8, 128), jnp.int32),
            pltpu.VMEM((CHIPS, 8, 128), jnp.int32),
            pltpu.VMEM((CHIPS, 128), jnp.int32),
            pltpu.SMEM((CHIPS, 128), jnp.int32),
            pltpu.VMEM((2, TILES, HEADS * TILE, 3 * KHALF), BF16),
            pltpu.VMEM((TILES, HEADS * TILE, 1), F32),
            pltpu.VMEM((TILES, HEADS * TILE, 1), F32),
            pltpu.VMEM((TILES, HEADS * TILE, DIM), F32),
            dma((4,)), dma, dma, dma, dma,
            dma((4,)), dma((4, NY)),
            dma((4,)), dma((4, 2, RING_STEPS, PIECES)),
            dma((4,)),
            dma((4,)), dma((4,)),
        ]
    )
    return pl.pallas_call(
        kernel,
        out_shape=jax.ShapeDtypeStruct(queries.shape, BF16),
        in_specs=[hbm] * 4,
        out_specs=hbm,
        scratch_shapes=scratch,
        compiler_params=pltpu.CompilerParams(
            collective_id=0, has_side_effects=True, vmem_limit_bytes=56 << 20),
        cost_estimate=pl.CostEstimate(flops=4 << 30, bytes_accessed=8 << 20, transcendentals=8 << 20),
        name="moba",
    )(queries, keys.reshape(view), values.reshape(view), selected.T)


def solution(mesh):
    spec = P(("node", "local"), None)
    return jax.shard_map(
        body, mesh=mesh, in_specs=(spec,) * 4, out_specs=spec, check_vma=False)
```

```python
import functools
import math

import jax
import jax.numpy as jnp
from jax import lax
from jax.experimental import pallas as pl
from jax.experimental.pallas import tpu as pltpu
from jax.sharding import PartitionSpec as P

MESH = pl.DeviceIdType.MESH
BF16 = jnp.bfloat16
F32 = jnp.float32

TILE = 128
BLOCK = 512
KHALF = BLOCK // 2
HEADS = 4
DIM = 128
NX, NY, NZ = 4, 4, 8
CHIPS = NX * NY
SLOTS = 16
ENTRIES = 24
TILES = 8
UNIT = CHIPS * 2
STORE = NZ * 2 * UNIT
PIECES = 4
PIECE = UNIT // PIECES
UP_STEPS, DOWN_STEPS = (4, 3) * (PIECES // 2), (3, 4) * (PIECES // 2)
OWN_EVERY = 0.5
RING_STEPS = 4
SCALE2 = math.log2(math.e) / math.sqrt(DIM)
DEAD = -1e30

ORDER = [
    (0, 1), (0, 3), (1, 0), (3, 0), (1, 1), (3, 3), (1, 3), (3, 1),
    (0, 2), (2, 0), (2, 2), (1, 2), (3, 2), (2, 1), (2, 3),
]


PLACE = {offset: 1 + i for i, offset in enumerate(ORDER)}
EARLY = 8
WIDTHS = (KHALF, EARLY * 16, KHALF - EARLY * 16)
LONG_FIRST = ((0, 2, 1, 3), (1, 3, 0, 2))


def device(z, y, x, c):
    return (z * NY + y, x * 2 + c)


def kernel(
    q_hbm, k_hbm, v_hbm, sel_hbm, out_ref,
    q_ref, k_ref, v_ref, sel_ref,
    st0, st1, st2, st3, sb0, sb1, sb2, sb3, rb0, rb1, rb2, rb3, rb4,
    emap, wanted, req, idxv, idxs, p0_ref, p1_ref, p2_ref, m_ref, l_ref, acc_ref,
    in_sem, rq_send, rq_recv, ix_sem, t_send, t_recv, z_send, z_recv, s_recv, g_send, g_recv,
):
    store = [st0, st1, st2, st3]
    outgoing = [sb0, sb1, sb2, sb3]
    arrived = [rb0, rb1, rb2, rb3]
    node = lax.axis_index("node")
    local = lax.axis_index("local")
    z, y, x, c = node // NY, node % NY, local // 2, local % 2
    chip = y * NX + x

    def partner(dy, dx):
        return device(z, (y + dy) % NY, (x + dx) % NX, c)

    above = device((z + 1) % NZ, y, x, c)
    below = device((z + NZ - 1) % NZ, y, x, c)
    sibling = device(z, y, x, 1 - c)

    loads = [
        pltpu.make_async_copy(src, dst, in_sem.at[i])
        for i, (src, dst) in enumerate(
            [(sel_hbm, sel_ref), (k_hbm, k_ref), (v_hbm, v_ref), (q_hbm, q_ref)])
    ]
    barrier = pltpu.get_barrier_semaphore()
    for dy, dx in ORDER:
        pl.semaphore_signal(barrier, inc=1, device_id=partner(dy, dx), device_id_type=MESH)
    for other in (above, below, sibling):
        pl.semaphore_signal(barrier, inc=1, device_id=other, device_id_type=MESH)

    for load in loads:
        load.start()

    loads[0].wait()
    entries = [sel_ref[j % 3, j // 3] for j in range(ENTRIES)]
    lane = lax.broadcasted_iota(jnp.int32, (8, 128), 1)
    ids = jnp.full((8, 128), z * (CHIPS * 4), jnp.int32)
    numbers = []
    count = jnp.int32(0)
    for j, entry in enumerate(entries):
        number, seen = count, entry < 0
        for i in range(j):
            same = entries[i] == entry
            number = jnp.where(same, numbers[i], number)
            seen = seen | same
        number = jnp.where(entry < 0, -1, number)
        count = jnp.where(seen, count, count + 1)
        numbers.append(number)
        emap[j] = number
        ids = jnp.where(lane == number, entry, ids)
    wanted[...] = ids

    loads[1].wait()
    pl.semaphore_wait(barrier, len(ORDER) + 3)

    def source(q, piece):
        ref = k_ref if q < 2 else v_ref
        return ref.at[:, piece, q % 2]

    def spread(q):
        for dy, dx in ORDER:
            to = ((y + dy) % NY) * NX + (x + dx) % NX
            offset = dy * NX + dx
            pltpu.make_async_remote_copy(
                source(q, to),
                store[q].at[pl.ds((c * NZ + z) * UNIT + offset * 2, 2)],
                t_send.at[q], t_recv.at[q, dy],
                device_id=partner(dy, dx), device_id_type=MESH,
            ).start()
        store[q][pl.ds((c * NZ + z) * UNIT, 2)] = source(q, chip)[...]

    def spread_wait(q, h):
        first = 2 if h == 0 else 0
        rest = store[q].at[pl.ds((c * NZ + z) * UNIT + h * PIECE + first, PIECE - first)]
        pltpu.make_async_copy(rest, rest, t_recv.at[q, h]).wait()

    def ask():
        for dy, dx in ORDER:
            pltpu.make_async_remote_copy(
                wanted, req.at[dy * NX + dx], rq_send, rq_recv,
                device_id=partner(dy, dx), device_id_type=MESH,
            ).start()
        req[0] = wanted[...]

    def places():
        rest = req.at[pl.ds(1, CHIPS - 1)]
        pltpu.make_async_copy(rest, rest, rq_recv).wait()
        ids = req[:, 0, :]
        offset_y = (y + NY - (ids // 16) % NY) % NY
        offset_x = (x + NX - (ids // 4) % NX) % NX
        idxv[...] = ((ids // 2) % 2 * NZ + ids // 64) * UNIT + (offset_y * NX + offset_x) * 2 + ids % 2
        pltpu.make_async_copy(idxv, idxs, ix_sem).start()

    def places_wait():
        pltpu.make_async_copy(idxv, idxs, ix_sem).wait()

    def piece(q, plane, core, h):
        return store[q].at[pl.ds((core * NZ + plane) * UNIT + h * PIECE, PIECE)]

    def up_copy(q, t, h):
        ref = piece(q, z - t, c, h)
        return pltpu.make_async_remote_copy(
            ref, ref, z_send.at[q], z_recv.at[q, 0, t, h],
            device_id=above, device_id_type=MESH,
        )

    def down_copy(q, t, h):
        ref = piece(q, (z + t) % NZ, c, h)
        return pltpu.make_async_remote_copy(
            ref, ref, z_send.at[q], z_recv.at[q, 1, t, h],
            device_id=below, device_id_type=MESH,
        )

    def across_copy(q, plane, h):
        ref = piece(q, plane, c, h)
        return pltpu.make_async_remote_copy(
            ref, ref, z_send.at[q], s_recv.at[q],
            device_id=sibling, device_id_type=MESH,
        )

    def sends_up(t):
        return (z - t >= 0) & (z < NZ - 1)

    def sends_down(t, h):
        return (z + t) % NZ < DOWN_STEPS[h]

    def gets_up(t):
        return z - 1 - t >= 0

    def gets_down(t, h):
        return (z + 1 + t) % NZ < DOWN_STEPS[h]

    spread_seen = set()

    def ring_step(q, t, h, way):
        if t == 0 and (q, h) not in spread_seen:
            spread_seen.add((q, h))
            spread_wait(q, h)
            across_copy(q, z, h).start()
        if way == 0:
            if 1 <= t <= UP_STEPS[h]:
                @pl.when(gets_up(t - 1))
                def _():
                    ref = piece(q, z - t, c, h)
                    pltpu.make_async_copy(ref, ref, z_recv.at[q, 0, t - 1, h]).wait()
            if t < UP_STEPS[h]:
                @pl.when(sends_up(t))
                def _():
                    up_copy(q, t, h).start()
            if 1 <= t <= UP_STEPS[h]:
                @pl.when(gets_up(t - 1))
                def _():
                    across_copy(q, z - t, h).start()
        else:
            if 1 <= t <= DOWN_STEPS[h]:
                @pl.when(gets_down(t - 1, h))
                def _():
                    ref = piece(q, (z + t) % NZ, c, h)
                    pltpu.make_async_copy(ref, ref, z_recv.at[q, 1, t - 1, h]).wait()
            if t < DOWN_STEPS[h]:
                @pl.when(sends_down(t, h))
                def _():
                    down_copy(q, t, h).start()
            if 1 <= t <= DOWN_STEPS[h]:
                @pl.when(gets_down(t - 1, h) & ((z + t) % NZ < z))
                def _():
                    across_copy(q, (z + t) % NZ, h).start()

    def across_wait(q):
        for plane in range(NZ):
            @pl.when(z == plane)
            def _():
                ref = store[q].at[pl.ds((1 - c) * NZ * UNIT, (plane + 1) * UNIT)]
                pltpu.make_async_copy(ref, ref, s_recv.at[q]).wait()

    def ring_drain(q):
        for plane in range(NZ):
            count = 0
            for h in range(PIECES):
                if plane < NZ - 1:
                    count += sum(plane - t >= 0 for t in range(UP_STEPS[h]))
                count += sum((plane + t) % NZ < DOWN_STEPS[h] for t in range(DOWN_STEPS[h]))
            tiles = count * PIECE + (plane + 1) * UNIT

            @pl.when(z == plane)
            def _():
                ref = store[q].at[pl.ds(0, tiles)]
                pltpu.make_async_copy(ref, ref, z_send.at[q]).wait()
        rest = store[q].at[pl.ds(0, UNIT - 2)]
        pltpu.make_async_copy(rest, rest, t_send.at[q]).wait()

    def landing(q, place):
        if q == 3 and place >= EARLY:
            return rb4.at[place - EARLY]
        return arrived[q].at[place]

    def gather(q, part):
        if part == 0:
            for s in range(SLOTS):
                arrived[q][0, s] = store[q][idxs[0, s]]
        for dy, dx in ORDER[part * 4:part * 4 + 4]:
            place = PLACE[dy, dx]
            asked = ((NY - dy) % NY) * NX + (NX - dx) % NX
            for s in range(SLOTS):
                outgoing[q][place, s] = store[q][idxs[asked, s]]
            pltpu.make_async_remote_copy(
                outgoing[q].at[place], landing(q, place),
                g_send.at[q], g_recv.at[q + 1 if q == 3 and place >= EARLY else q],
                device_id=partner(dy, dx), device_id_type=MESH,
            ).start()

    def gather_wait(q):
        if q == 4:
            rest = rb4
        else:
            rest = arrived[q].at[pl.ds(1, (EARLY if q == 3 else CHIPS) - 1)]
        pltpu.make_async_copy(rest, rest, g_recv.at[q]).wait()

    def stacked(t):
        rows = pl.ds(t * TILE, TILE)
        return jnp.concatenate([q_ref[rows, h * DIM:(h + 1) * DIM] for h in range(HEADS)], axis=0)

    def scores(a, b):
        return lax.dot_general(a, b, (((1,), (1,)), ((), ())), preferred_element_type=F32)

    def own(t):
        block, r = t // (BLOCK // TILE), t % (BLOCK // TILE)
        width = (r + 1) * TILE
        keys = k_ref[block].reshape(BLOCK, DIM)[:width]
        vals = v_ref[block].reshape(BLOCK, DIM)[:width]
        s = scores(stacked(t), keys)
        row = lax.broadcasted_iota(jnp.int32, s.shape, 0) % TILE + r * TILE
        col = lax.broadcasted_iota(jnp.int32, s.shape, 1)
        s = jnp.where(col <= row, s, -jnp.inf)
        m = jnp.max(s, axis=1, keepdims=True)
        p = jnp.exp2(s * SCALE2 - m * SCALE2)
        m_ref[t] = m
        l_ref[t] = jnp.sum(p, axis=1, keepdims=True)
        acc_ref[t] = jnp.dot(p.astype(BF16), vals, preferred_element_type=F32)

    def slot_of(t, e):
        entry = emap[t * 3 + e]
        return jnp.maximum(entry, 0), jnp.where(entry < 0, DEAD, 0.0).astype(F32)

    def remote_keys(t, carry):
        queries = stacked(t)
        m_own = m_ref[t]
        m = m_own
        parts = []
        for e in range(3):
            slot, bias = slot_of(t, e)
            keys = jnp.concatenate(
                [rb0[:, slot].reshape(KHALF, DIM), rb1[:, slot].reshape(KHALF, DIM)], axis=0)
            s = scores(queries, keys)
            m = jnp.maximum(m, jnp.max(s, axis=1, keepdims=True) + bias)
            parts.append((s, bias))
        m2 = m * SCALE2
        alpha = jnp.exp2(m_own * SCALE2 - m2)
        total = l_ref[t] * alpha
        for e, (s, bias) in enumerate(parts):
            p = jnp.exp2(s * SCALE2 - (m2 - bias))
            total = total + jnp.sum(p, axis=1, keepdims=True)
            p = p.astype(BF16)
            first = 0
            for p_ref, width in zip((p0_ref, p1_ref, p2_ref), WIDTHS):
                p_ref[t, :, e * width:(e + 1) * width] = p[:, first:first + width]
                first += width
        l_ref[t] = 1.0 / total
        acc_ref[t] = acc_ref[t] * alpha
        return carry

    def remote_values(stage):
        ref = (rb2, rb3, rb4)[stage]
        p_ref = (p0_ref, p1_ref, p2_ref)[stage]

        def one(t):
            slots = [slot_of(t, e)[0] for e in range(3)]
            vals = jnp.concatenate([ref[:, slot].reshape(WIDTHS[stage], DIM) for slot in slots], axis=0)
            acc = acc_ref[t] + jnp.dot(p_ref[t], vals, preferred_element_type=F32)
            if stage == 2:
                normed = (acc * l_ref[t]).astype(BF16)
                rows = pl.ds(pl.multiple_of(t * TILE, TILE), TILE)
                for h in range(HEADS):
                    out_ref[rows, h * DIM:(h + 1) * DIM] = normed[h * TILE:(h + 1) * TILE]
            else:
                acc_ref[t] = acc

        def step(pair, carry):
            one(pair * 2)
            one(pair * 2 + 1)
            return carry

        lax.fori_loop(0, TILES // 2, step, 0)

    spread(0)
    ask()
    spread(1)
    for i in range(PIECES):
        for way in range(2):
            ring_step(0, 0, LONG_FIRST[way][i], way)
    loads[2].wait()
    spread(2)
    spread(3)
    loads[3].wait()

    events = []
    for q in range(4):
        begin = 3.5 * q
        for i in range(PIECES):
            for way in range(2):
                for t in range(0 if q else 1, RING_STEPS + 1):
                    events.append((begin + t + i / PIECES, functools.partial(ring_step, q, t, LONG_FIRST[way][i], way)))
        events.append((begin + 4.3, functools.partial(across_wait, q)))
        for part in range(4):
            events.append((begin + 4.31 + 0.5 * part * (q < 3), functools.partial(gather, q, part)))
    for t in range(TILES):
        events.append((0.9 + OWN_EVERY * t, functools.partial(own, t)))
    events.append((2.1, places))
    events.append((2.9, places_wait))
    for _, task in sorted(events, key=lambda event: event[0]):
        task()

    gather_wait(0)
    gather_wait(1)
    lax.fori_loop(0, TILES, remote_keys, 0)
    rest = req.at[pl.ds(1, CHIPS - 1)]
    pltpu.make_async_copy(rest, rest, rq_send).wait()
    for q in range(4):
        ring_drain(q)
        if q < 3:
            rest = outgoing[q].at[pl.ds(1, CHIPS - 1)]
            pltpu.make_async_copy(rest, rest, g_send.at[q]).wait()
    gather_wait(2)
    remote_values(0)
    gather_wait(3)
    remote_values(1)
    gather_wait(4)
    remote_values(2)

    rest = outgoing[3].at[pl.ds(1, CHIPS - 1)]
    pltpu.make_async_copy(rest, rest, g_send.at[3]).wait()


def body(queries, keys, values, selected):
    tokens = keys.shape[0]
    view = (tokens // BLOCK, CHIPS, 2, 16, DIM)
    hbm = pl.BlockSpec(memory_space=pl.ANY)
    dma = pltpu.SemaphoreType.DMA
    scratch = (
        [
            pltpu.VMEM(queries.shape, BF16),
            pltpu.VMEM(view, BF16),
            pltpu.VMEM(view, BF16),
            pltpu.SMEM(selected.shape[::-1], jnp.int32),
        ]
        + [pltpu.VMEM((STORE, 16, DIM), BF16)] * 4
        + [pltpu.VMEM((CHIPS, SLOTS, 16, DIM), BF16)] * 7
        + [pltpu.VMEM((EARLY, SLOTS, 16, DIM), BF16), pltpu.VMEM((CHIPS - EARLY, SLOTS, 16, DIM), BF16)]
        + [
            pltpu.SMEM((ENTRIES,), jnp.int32),
            pltpu.VMEM((8, 128), jnp.int32),
            pltpu.VMEM((CHIPS, 8, 128), jnp.int32),
            pltpu.VMEM((CHIPS, 128), jnp.int32),
            pltpu.SMEM((CHIPS, 128), jnp.int32),
            *[pltpu.VMEM((TILES, HEADS * TILE, 3 * width), BF16) for width in WIDTHS],
            pltpu.VMEM((TILES, HEADS * TILE, 1), F32),
            pltpu.VMEM((TILES, HEADS * TILE, 1), F32),
            pltpu.VMEM((TILES, HEADS * TILE, DIM), F32),
            dma((4,)), dma, dma, dma,
            dma((4,)), dma((4, NY)),
            dma((4,)), dma((4, 2, RING_STEPS, PIECES)),
            dma((4,)),
            dma((4,)), dma((5,)),
        ]
    )
    return pl.pallas_call(
        kernel,
        out_shape=pltpu.VMEM(queries.shape, BF16),
        in_specs=[hbm] * 4,
        out_specs=pl.BlockSpec(memory_space=pltpu.VMEM),
        scratch_shapes=scratch,
        compiler_params=pltpu.CompilerParams(
            collective_id=0, has_side_effects=True, vmem_limit_bytes=56 << 20),
        cost_estimate=pl.CostEstimate(flops=4 << 30, bytes_accessed=8 << 20, transcendentals=8 << 20),
        name="moba",
    )(queries, keys.reshape(view), values.reshape(view), selected.T)


def solution(mesh):
    spec = P(("node", "local"), None)
    return jax.shard_map(
        body, mesh=mesh, in_specs=(spec,) * 4, out_specs=spec, check_vma=False)
```

```python
import functools
import math

import jax
import jax.numpy as jnp
from jax import lax
from jax.experimental import pallas as pl
from jax.experimental.pallas import tpu as pltpu
from jax.sharding import PartitionSpec as P

MESH = pl.DeviceIdType.MESH
BF16 = jnp.bfloat16
F32 = jnp.float32

TILE = 128
BLOCK = 512
KHALF = BLOCK // 2
HEADS = 4
DIM = 128
NX, NY, NZ = 4, 4, 8
CHIPS = NX * NY
SLOTS = 16
ENTRIES = 24
TILES = 8
UNIT = CHIPS * 2
STORE = NZ * 2 * UNIT
PIECES = 4
PIECE = UNIT // PIECES
UP_STEPS, DOWN_STEPS = (4, 3) * (PIECES // 2), (3, 4) * (PIECES // 2)
OWN_EVERY = 0.5
KEYS_EARLY, KEYS_AT, KEYS_EVERY = 3, 13.4, 0.45
RING_STEPS = 4
SCALE2 = math.log2(math.e) / math.sqrt(DIM)
DEAD = -1e30

ORDER = [
    (0, 1), (0, 3), (1, 0), (3, 0), (1, 1), (3, 3), (1, 3), (3, 1),
    (0, 2), (2, 0), (2, 2), (1, 2), (3, 2), (2, 1), (2, 3),
]


PLACE = {offset: 1 + i for i, offset in enumerate(ORDER)}
EARLY = 8
WIDTHS = (KHALF, EARLY * 16, KHALF - EARLY * 16)
LONG_FIRST = ((0, 2, 1, 3), (1, 3, 0, 2))


def device(z, y, x, c):
    return (z * NY + y, x * 2 + c)


def kernel(
    q_hbm, k_hbm, v_hbm, sel_hbm, out_ref,
    q_ref, k_ref, v_ref, sel_ref,
    st0, st1, st2, st3, sb0, sb1, sb2, sb3, rb0, rb1, rb2, rb3, rb4,
    emap, wanted, req, idxv, idxs, p0_ref, p1_ref, p2_ref, m_ref, l_ref, acc_ref,
    in_sem, rq_send, rq_recv, ix_sem, t_send, t_recv, z_send, z_recv, s_recv, g_send, g_recv,
):
    store = [st0, st1, st2, st3]
    outgoing = [sb0, sb1, sb2, sb3]
    arrived = [rb0, rb1, rb2, rb3]
    node = lax.axis_index("node")
    local = lax.axis_index("local")
    z, y, x, c = node // NY, node % NY, local // 2, local % 2
    chip = y * NX + x

    def partner(dy, dx):
        return device(z, (y + dy) % NY, (x + dx) % NX, c)

    above = device((z + 1) % NZ, y, x, c)
    below = device((z + NZ - 1) % NZ, y, x, c)
    sibling = device(z, y, x, 1 - c)

    loads = [
        pltpu.make_async_copy(src, dst, in_sem.at[i])
        for i, (src, dst) in enumerate(
            [(sel_hbm, sel_ref), (k_hbm, k_ref), (v_hbm, v_ref), (q_hbm, q_ref)])
    ]
    barrier = pltpu.get_barrier_semaphore()
    for dy, dx in ORDER:
        pl.semaphore_signal(barrier, inc=1, device_id=partner(dy, dx), device_id_type=MESH)
    for other in (above, below, sibling):
        pl.semaphore_signal(barrier, inc=1, device_id=other, device_id_type=MESH)

    for load in loads:
        load.start()

    loads[0].wait()
    entries = [sel_ref[j % 3, j // 3] for j in range(ENTRIES)]
    lane = lax.broadcasted_iota(jnp.int32, (8, 128), 1)
    ids = jnp.full((8, 128), z * (CHIPS * 4), jnp.int32)
    numbers = []
    count = jnp.int32(0)
    for j, entry in enumerate(entries):
        number, seen = count, entry < 0
        for i in range(j):
            same = entries[i] == entry
            number = jnp.where(same, numbers[i], number)
            seen = seen | same
        number = jnp.where(entry < 0, -1, number)
        count = jnp.where(seen, count, count + 1)
        numbers.append(number)
        emap[j] = number
        ids = jnp.where(lane == number, entry, ids)
    wanted[...] = ids

    loads[1].wait()
    pl.semaphore_wait(barrier, len(ORDER) + 3)

    def source(q, piece):
        ref = k_ref if q < 2 else v_ref
        return ref.at[:, piece, q % 2]

    def spread(q):
        for dy, dx in ORDER:
            to = ((y + dy) % NY) * NX + (x + dx) % NX
            offset = dy * NX + dx
            pltpu.make_async_remote_copy(
                source(q, to),
                store[q].at[pl.ds((c * NZ + z) * UNIT + offset * 2, 2)],
                t_send.at[q], t_recv.at[q, dy],
                device_id=partner(dy, dx), device_id_type=MESH,
            ).start()
        store[q][pl.ds((c * NZ + z) * UNIT, 2)] = source(q, chip)[...]

    def spread_wait(q, h):
        first = 2 if h == 0 else 0
        rest = store[q].at[pl.ds((c * NZ + z) * UNIT + h * PIECE + first, PIECE - first)]
        pltpu.make_async_copy(rest, rest, t_recv.at[q, h]).wait()

    def ask():
        for dy, dx in ORDER:
            pltpu.make_async_remote_copy(
                wanted, req.at[dy * NX + dx], rq_send, rq_recv,
                device_id=partner(dy, dx), device_id_type=MESH,
            ).start()
        req[0] = wanted[...]

    def places():
        rest = req.at[pl.ds(1, CHIPS - 1)]
        pltpu.make_async_copy(rest, rest, rq_recv).wait()
        ids = req[:, 0, :]
        offset_y = (y + NY - (ids // 16) % NY) % NY
        offset_x = (x + NX - (ids // 4) % NX) % NX
        idxv[...] = ((ids // 2) % 2 * NZ + ids // 64) * UNIT + (offset_y * NX + offset_x) * 2 + ids % 2
        pltpu.make_async_copy(idxv, idxs, ix_sem).start()

    def places_wait():
        pltpu.make_async_copy(idxv, idxs, ix_sem).wait()

    def piece(q, plane, core, h):
        return store[q].at[pl.ds((core * NZ + plane) * UNIT + h * PIECE, PIECE)]

    def up_copy(q, t, h):
        ref = piece(q, z - t, c, h)
        return pltpu.make_async_remote_copy(
            ref, ref, z_send.at[q], z_recv.at[q, 0, t, h],
            device_id=above, device_id_type=MESH,
        )

    def down_copy(q, t, h):
        ref = piece(q, (z + t) % NZ, c, h)
        return pltpu.make_async_remote_copy(
            ref, ref, z_send.at[q], z_recv.at[q, 1, t, h],
            device_id=below, device_id_type=MESH,
        )

    def across_copy(q, plane, h):
        ref = piece(q, plane, c, h)
        return pltpu.make_async_remote_copy(
            ref, ref, z_send.at[q], s_recv.at[q],
            device_id=sibling, device_id_type=MESH,
        )

    def sends_up(t):
        return (z - t >= 0) & (z < NZ - 1)

    def sends_down(t, h):
        return (z + t) % NZ < DOWN_STEPS[h]

    def gets_up(t):
        return z - 1 - t >= 0

    def gets_down(t, h):
        return (z + 1 + t) % NZ < DOWN_STEPS[h]

    spread_seen = set()

    def ring_step(q, t, h, way):
        if t == 0 and (q, h) not in spread_seen:
            spread_seen.add((q, h))
            spread_wait(q, h)
            across_copy(q, z, h).start()
        if way == 0:
            if 1 <= t <= UP_STEPS[h]:
                @pl.when(gets_up(t - 1))
                def _():
                    ref = piece(q, z - t, c, h)
                    pltpu.make_async_copy(ref, ref, z_recv.at[q, 0, t - 1, h]).wait()
            if t < UP_STEPS[h]:
                @pl.when(sends_up(t))
                def _():
                    up_copy(q, t, h).start()
            if 1 <= t <= UP_STEPS[h]:
                @pl.when(gets_up(t - 1))
                def _():
                    across_copy(q, z - t, h).start()
        else:
            if 1 <= t <= DOWN_STEPS[h]:
                @pl.when(gets_down(t - 1, h))
                def _():
                    ref = piece(q, (z + t) % NZ, c, h)
                    pltpu.make_async_copy(ref, ref, z_recv.at[q, 1, t - 1, h]).wait()
            if t < DOWN_STEPS[h]:
                @pl.when(sends_down(t, h))
                def _():
                    down_copy(q, t, h).start()
            if 1 <= t <= DOWN_STEPS[h]:
                @pl.when(gets_down(t - 1, h) & ((z + t) % NZ < z))
                def _():
                    across_copy(q, (z + t) % NZ, h).start()

    def across_wait(q):
        for plane in range(NZ):
            @pl.when(z == plane)
            def _():
                ref = store[q].at[pl.ds((1 - c) * NZ * UNIT, (plane + 1) * UNIT)]
                pltpu.make_async_copy(ref, ref, s_recv.at[q]).wait()

    def ring_drain(q):
        for plane in range(NZ):
            count = 0
            for h in range(PIECES):
                if plane < NZ - 1:
                    count += sum(plane - t >= 0 for t in range(UP_STEPS[h]))
                count += sum((plane + t) % NZ < DOWN_STEPS[h] for t in range(DOWN_STEPS[h]))
            tiles = count * PIECE + (plane + 1) * UNIT

            @pl.when(z == plane)
            def _():
                ref = store[q].at[pl.ds(0, tiles)]
                pltpu.make_async_copy(ref, ref, z_send.at[q]).wait()
        rest = store[q].at[pl.ds(0, UNIT - 2)]
        pltpu.make_async_copy(rest, rest, t_send.at[q]).wait()

    def landing(q, place):
        if q == 3 and place >= EARLY:
            return rb4.at[place - EARLY]
        return arrived[q].at[place]

    def gather(q, part):
        if part == 0:
            for s in range(SLOTS):
                arrived[q][0, s] = store[q][idxs[0, s]]
        for dy, dx in ORDER[part * 4:part * 4 + 4]:
            place = PLACE[dy, dx]
            asked = ((NY - dy) % NY) * NX + (NX - dx) % NX
            for s in range(SLOTS):
                outgoing[q][place, s] = store[q][idxs[asked, s]]
            pltpu.make_async_remote_copy(
                outgoing[q].at[place], landing(q, place),
                g_send.at[q], g_recv.at[q + 1 if q == 3 and place >= EARLY else q],
                device_id=partner(dy, dx), device_id_type=MESH,
            ).start()

    def gather_wait(q):
        if q == 4:
            rest = rb4
        else:
            rest = arrived[q].at[pl.ds(1, (EARLY if q == 3 else CHIPS) - 1)]
        pltpu.make_async_copy(rest, rest, g_recv.at[q]).wait()

    def stacked(t):
        rows = pl.ds(t * TILE, TILE)
        return jnp.concatenate([q_ref[rows, h * DIM:(h + 1) * DIM] for h in range(HEADS)], axis=0)

    def scores(a, b):
        return lax.dot_general(a, b, (((1,), (1,)), ((), ())), preferred_element_type=F32)

    def own(t):
        block, r = t // (BLOCK // TILE), t % (BLOCK // TILE)
        width = (r + 1) * TILE
        keys = k_ref[block].reshape(BLOCK, DIM)[:width]
        vals = v_ref[block].reshape(BLOCK, DIM)[:width]
        s = scores(stacked(t), keys)
        row = lax.broadcasted_iota(jnp.int32, s.shape, 0) % TILE + r * TILE
        col = lax.broadcasted_iota(jnp.int32, s.shape, 1)
        s = jnp.where(col <= row, s, -jnp.inf)
        m = jnp.max(s, axis=1, keepdims=True)
        p = jnp.exp2(s * SCALE2 - m * SCALE2)
        m_ref[t] = m
        l_ref[t] = jnp.sum(p, axis=1, keepdims=True)
        acc_ref[t] = jnp.dot(p.astype(BF16), vals, preferred_element_type=F32)

    def slot_of(t, e):
        entry = emap[t * 3 + e]
        return jnp.maximum(entry, 0), jnp.where(entry < 0, DEAD, 0.0).astype(F32)

    def remote_keys(t, carry):
        queries = stacked(t)
        m_own = m_ref[t]
        m = m_own
        parts = []
        for e in range(3):
            slot, bias = slot_of(t, e)
            keys = jnp.concatenate(
                [rb0[:, slot].reshape(KHALF, DIM), rb1[:, slot].reshape(KHALF, DIM)], axis=0)
            s = scores(queries, keys)
            m = jnp.maximum(m, jnp.max(s, axis=1, keepdims=True) + bias)
            parts.append((s, bias))
        m2 = m * SCALE2
        alpha = jnp.exp2(m_own * SCALE2 - m2)
        total = l_ref[t] * alpha
        for e, (s, bias) in enumerate(parts):
            p = jnp.exp2(s * SCALE2 - (m2 - bias))
            total = total + jnp.sum(p, axis=1, keepdims=True)
            p = p.astype(BF16)
            first = 0
            for p_ref, width in zip((p0_ref, p1_ref, p2_ref), WIDTHS):
                p_ref[t, :, e * width:(e + 1) * width] = p[:, first:first + width]
                first += width
        l_ref[t] = 1.0 / total
        acc_ref[t] = acc_ref[t] * alpha
        return carry

    def remote_values(stage):
        ref = (rb2, rb3, rb4)[stage]
        p_ref = (p0_ref, p1_ref, p2_ref)[stage]

        def one(t):
            slots = [slot_of(t, e)[0] for e in range(3)]
            vals = jnp.concatenate([ref[:, slot].reshape(WIDTHS[stage], DIM) for slot in slots], axis=0)
            acc = acc_ref[t] + jnp.dot(p_ref[t], vals, preferred_element_type=F32)
            if stage == 2:
                normed = (acc * l_ref[t]).astype(BF16)
                rows = pl.ds(pl.multiple_of(t * TILE, TILE), TILE)
                for h in range(HEADS):
                    out_ref[rows, h * DIM:(h + 1) * DIM] = normed[h * TILE:(h + 1) * TILE]
            else:
                acc_ref[t] = acc

        def step(pair, carry):
            one(pair * 2)
            one(pair * 2 + 1)
            return carry

        lax.fori_loop(0, TILES // 2, step, 0)

    spread(0)
    ask()
    spread(1)
    for i in range(PIECES):
        for way in range(2):
            ring_step(0, 0, LONG_FIRST[way][i], way)
    loads[2].wait()
    spread(2)
    spread(3)
    loads[3].wait()

    events = []
    for q in range(4):
        begin = 3.5 * q
        for i in range(PIECES):
            for way in range(2):
                for t in range(0 if q else 1, RING_STEPS + 1):
                    events.append((begin + t + i / PIECES, functools.partial(ring_step, q, t, LONG_FIRST[way][i], way)))
        events.append((begin + 4.3, functools.partial(across_wait, q)))
        for part in range(4):
            events.append((begin + 4.31 + 0.5 * part * (q < 3), functools.partial(gather, q, part)))
    for t in range(TILES):
        events.append((0.9 + OWN_EVERY * t, functools.partial(own, t)))
    events.append((KEYS_AT - 0.02, functools.partial(gather_wait, 0)))
    events.append((KEYS_AT - 0.01, functools.partial(gather_wait, 1)))
    for t in range(KEYS_EARLY):
        events.append((KEYS_AT + KEYS_EVERY * t, functools.partial(remote_keys, t, 0)))
    events.append((2.1, places))
    events.append((2.9, places_wait))
    for _, task in sorted(events, key=lambda event: event[0]):
        task()

    lax.fori_loop(KEYS_EARLY, TILES, remote_keys, 0)
    rest = req.at[pl.ds(1, CHIPS - 1)]
    pltpu.make_async_copy(rest, rest, rq_send).wait()
    for q in range(4):
        ring_drain(q)
        if q < 3:
            rest = outgoing[q].at[pl.ds(1, CHIPS - 1)]
            pltpu.make_async_copy(rest, rest, g_send.at[q]).wait()
    gather_wait(2)
    remote_values(0)
    gather_wait(3)
    remote_values(1)
    gather_wait(4)
    remote_values(2)

    rest = outgoing[3].at[pl.ds(1, CHIPS - 1)]
    pltpu.make_async_copy(rest, rest, g_send.at[3]).wait()


def body(queries, keys, values, selected):
    tokens = keys.shape[0]
    view = (tokens // BLOCK, CHIPS, 2, 16, DIM)
    hbm = pl.BlockSpec(memory_space=pl.ANY)
    dma = pltpu.SemaphoreType.DMA
    scratch = (
        [
            pltpu.VMEM(queries.shape, BF16),
            pltpu.VMEM(view, BF16),
            pltpu.VMEM(view, BF16),
            pltpu.SMEM(selected.shape[::-1], jnp.int32),
        ]
        + [pltpu.VMEM((STORE, 16, DIM), BF16)] * 4
        + [pltpu.VMEM((CHIPS, SLOTS, 16, DIM), BF16)] * 7
        + [pltpu.VMEM((EARLY, SLOTS, 16, DIM), BF16), pltpu.VMEM((CHIPS - EARLY, SLOTS, 16, DIM), BF16)]
        + [
            pltpu.SMEM((ENTRIES,), jnp.int32),
            pltpu.VMEM((8, 128), jnp.int32),
            pltpu.VMEM((CHIPS, 8, 128), jnp.int32),
            pltpu.VMEM((CHIPS, 128), jnp.int32),
            pltpu.SMEM((CHIPS, 128), jnp.int32),
            *[pltpu.VMEM((TILES, HEADS * TILE, 3 * width), BF16) for width in WIDTHS],
            pltpu.VMEM((TILES, HEADS * TILE, 1), F32),
            pltpu.VMEM((TILES, HEADS * TILE, 1), F32),
            pltpu.VMEM((TILES, HEADS * TILE, DIM), F32),
            dma((4,)), dma, dma, dma,
            dma((4,)), dma((4, NY)),
            dma((4,)), dma((4, 2, RING_STEPS, PIECES)),
            dma((4,)),
            dma((4,)), dma((5,)),
        ]
    )
    return pl.pallas_call(
        kernel,
        out_shape=pltpu.VMEM(queries.shape, BF16),
        in_specs=[hbm] * 4,
        out_specs=pl.BlockSpec(memory_space=pltpu.VMEM),
        scratch_shapes=scratch,
        compiler_params=pltpu.CompilerParams(
            collective_id=0, has_side_effects=True, vmem_limit_bytes=56 << 20),
        cost_estimate=pl.CostEstimate(flops=4 << 30, bytes_accessed=8 << 20, transcendentals=8 << 20),
        name="moba",
    )(queries, keys.reshape(view), values.reshape(view), selected.T)


def solution(mesh):
    spec = P(("node", "local"), None)
    return jax.shard_map(
        body, mesh=mesh, in_specs=(spec,) * 4, out_specs=spec, check_vma=False)
```

```python
import functools
import math

import jax
import jax.numpy as jnp
from jax import lax
from jax.experimental import pallas as pl
from jax.experimental.pallas import tpu as pltpu
from jax.sharding import PartitionSpec as P

MESH = pl.DeviceIdType.MESH
BF16 = jnp.bfloat16
F32 = jnp.float32

TILE = 128
BLOCK = 512
KHALF = BLOCK // 2
HEADS = 4
DIM = 128
NX, NY, NZ = 4, 4, 8
CHIPS = NX * NY
SLOTS = 16
ENTRIES = 24
TILES = 8
UNIT = CHIPS * 2
STORE = NZ * 2 * UNIT
PIECES = 4
PIECE = UNIT // PIECES
UP_STEPS, DOWN_STEPS = (4, 3) * (PIECES // 2), (3, 4) * (PIECES // 2)
OWN_EVERY = 0.5
KEYS_EARLY, KEYS_AT, KEYS_EVERY = 2, 13.4, 0.6
RING_STEPS = 4
SCALE2 = math.log2(math.e) / math.sqrt(DIM)
DEAD = -1e30

ORDER = [
    (0, 1), (0, 3), (1, 0), (3, 0), (1, 1), (3, 3), (1, 3), (3, 1),
    (0, 2), (2, 0), (2, 2), (1, 2), (3, 2), (2, 1), (2, 3),
]


PLACE = {offset: 1 + i for i, offset in enumerate(ORDER)}
EARLY = 8
WIDTHS = (KHALF, EARLY * 16, KHALF - EARLY * 16)
LONG_FIRST = ((0, 2, 1, 3), (1, 3, 0, 2))


def device(z, y, x, c):
    return (z * NY + y, x * 2 + c)


def kernel(
    q_hbm, k_hbm, v_hbm, sel_hbm, out_ref,
    q_ref, k_ref, v_ref, sel_ref,
    st0, st1, st2, st3, sb0, sb1, sb2, sb3, rb0, rb1, rb2, rb3, rb4,
    emap, wanted, req, idxv, idxs, p0_ref, p1_ref, p2_ref, m_ref, l_ref, acc_ref,
    in_sem, rq_send, rq_recv, ix_sem, t_send, t_recv, z_send, z_recv, s_recv, g_send, g_recv,
):
    store = [st0, st1, st2, st3]
    outgoing = [sb0, sb1, sb2, sb3]
    arrived = [rb0, rb1, rb2, rb3]
    node = lax.axis_index("node")
    local = lax.axis_index("local")
    z, y, x, c = node // NY, node % NY, local // 2, local % 2
    chip = y * NX + x

    def partner(dy, dx):
        return device(z, (y + dy) % NY, (x + dx) % NX, c)

    above = device((z + 1) % NZ, y, x, c)
    below = device((z + NZ - 1) % NZ, y, x, c)
    sibling = device(z, y, x, 1 - c)

    loads = [
        pltpu.make_async_copy(src, dst, in_sem.at[i])
        for i, (src, dst) in enumerate(
            [(sel_hbm, sel_ref), (k_hbm, k_ref), (v_hbm, v_ref), (q_hbm, q_ref)])
    ]
    barrier = pltpu.get_barrier_semaphore()
    for dy, dx in ORDER:
        pl.semaphore_signal(barrier, inc=1, device_id=partner(dy, dx), device_id_type=MESH)
    for other in (above, below, sibling):
        pl.semaphore_signal(barrier, inc=1, device_id=other, device_id_type=MESH)

    for load in loads:
        load.start()

    loads[0].wait()
    entries = [sel_ref[j % 3, j // 3] for j in range(ENTRIES)]
    lane = lax.broadcasted_iota(jnp.int32, (8, 128), 1)
    ids = jnp.full((8, 128), z * (CHIPS * 4), jnp.int32)
    numbers = []
    count = jnp.int32(0)
    for j, entry in enumerate(entries):
        number, seen = count, entry < 0
        for i in range(j):
            same = entries[i] == entry
            number = jnp.where(same, numbers[i], number)
            seen = seen | same
        number = jnp.where(entry < 0, -1, number)
        count = jnp.where(seen, count, count + 1)
        numbers.append(number)
        emap[j] = number
        ids = jnp.where(lane == number, entry, ids)
    wanted[...] = ids

    loads[1].wait()
    pl.semaphore_wait(barrier, len(ORDER) + 3)

    def source(q, piece):
        ref = k_ref if q < 2 else v_ref
        return ref.at[:, piece, q % 2]

    def spread(q):
        for dy, dx in ORDER:
            to = ((y + dy) % NY) * NX + (x + dx) % NX
            offset = dy * NX + dx
            pltpu.make_async_remote_copy(
                source(q, to),
                store[q].at[pl.ds((c * NZ + z) * UNIT + offset * 2, 2)],
                t_send.at[q], t_recv.at[q, dy],
                device_id=partner(dy, dx), device_id_type=MESH,
            ).start()
        store[q][pl.ds((c * NZ + z) * UNIT, 2)] = source(q, chip)[...]

    def spread_wait(q, h):
        first = 2 if h == 0 else 0
        rest = store[q].at[pl.ds((c * NZ + z) * UNIT + h * PIECE + first, PIECE - first)]
        pltpu.make_async_copy(rest, rest, t_recv.at[q, h]).wait()

    def ask():
        for dy, dx in ORDER:
            pltpu.make_async_remote_copy(
                wanted, req.at[dy * NX + dx], rq_send, rq_recv,
                device_id=partner(dy, dx), device_id_type=MESH,
            ).start()
        req[0] = wanted[...]

    def places():
        rest = req.at[pl.ds(1, CHIPS - 1)]
        pltpu.make_async_copy(rest, rest, rq_recv).wait()
        ids = req[:, 0, :]
        offset_y = (y + NY - (ids // 16) % NY) % NY
        offset_x = (x + NX - (ids // 4) % NX) % NX
        idxv[...] = ((ids // 2) % 2 * NZ + ids // 64) * UNIT + (offset_y * NX + offset_x) * 2 + ids % 2
        pltpu.make_async_copy(idxv, idxs, ix_sem).start()

    def places_wait():
        pltpu.make_async_copy(idxv, idxs, ix_sem).wait()

    def piece(q, plane, core, h):
        return store[q].at[pl.ds((core * NZ + plane) * UNIT + h * PIECE, PIECE)]

    def up_copy(q, t, h):
        ref = piece(q, z - t, c, h)
        return pltpu.make_async_remote_copy(
            ref, ref, z_send.at[q], z_recv.at[q, 0, t, h],
            device_id=above, device_id_type=MESH,
        )

    def down_copy(q, t, h):
        ref = piece(q, (z + t) % NZ, c, h)
        return pltpu.make_async_remote_copy(
            ref, ref, z_send.at[q], z_recv.at[q, 1, t, h],
            device_id=below, device_id_type=MESH,
        )

    def across_copy(q, plane, h):
        ref = piece(q, plane, c, h)
        return pltpu.make_async_remote_copy(
            ref, ref, z_send.at[q], s_recv.at[q],
            device_id=sibling, device_id_type=MESH,
        )

    def sends_up(t):
        return (z - t >= 0) & (z < NZ - 1)

    def sends_down(t, h):
        return (z + t) % NZ < DOWN_STEPS[h]

    def gets_up(t):
        return z - 1 - t >= 0

    def gets_down(t, h):
        return (z + 1 + t) % NZ < DOWN_STEPS[h]

    spread_seen = set()

    def ring_step(q, t, h, way):
        if t == 0 and (q, h) not in spread_seen:
            spread_seen.add((q, h))
            spread_wait(q, h)
            across_copy(q, z, h).start()
        if way == 0:
            if 1 <= t <= UP_STEPS[h]:
                @pl.when(gets_up(t - 1))
                def _():
                    ref = piece(q, z - t, c, h)
                    pltpu.make_async_copy(ref, ref, z_recv.at[q, 0, t - 1, h]).wait()
            if t < UP_STEPS[h]:
                @pl.when(sends_up(t))
                def _():
                    up_copy(q, t, h).start()
            if 1 <= t <= UP_STEPS[h]:
                @pl.when(gets_up(t - 1))
                def _():
                    across_copy(q, z - t, h).start()
        else:
            if 1 <= t <= DOWN_STEPS[h]:
                @pl.when(gets_down(t - 1, h))
                def _():
                    ref = piece(q, (z + t) % NZ, c, h)
                    pltpu.make_async_copy(ref, ref, z_recv.at[q, 1, t - 1, h]).wait()
            if t < DOWN_STEPS[h]:
                @pl.when(sends_down(t, h))
                def _():
                    down_copy(q, t, h).start()
            if 1 <= t <= DOWN_STEPS[h]:
                @pl.when(gets_down(t - 1, h) & ((z + t) % NZ < z))
                def _():
                    across_copy(q, (z + t) % NZ, h).start()

    def across_wait(q):
        for plane in range(NZ):
            @pl.when(z == plane)
            def _():
                ref = store[q].at[pl.ds((1 - c) * NZ * UNIT, (plane + 1) * UNIT)]
                pltpu.make_async_copy(ref, ref, s_recv.at[q]).wait()

    def ring_drain(q):
        for plane in range(NZ):
            count = 0
            for h in range(PIECES):
                if plane < NZ - 1:
                    count += sum(plane - t >= 0 for t in range(UP_STEPS[h]))
                count += sum((plane + t) % NZ < DOWN_STEPS[h] for t in range(DOWN_STEPS[h]))
            tiles = count * PIECE + (plane + 1) * UNIT

            @pl.when(z == plane)
            def _():
                ref = store[q].at[pl.ds(0, tiles)]
                pltpu.make_async_copy(ref, ref, z_send.at[q]).wait()
        rest = store[q].at[pl.ds(0, UNIT - 2)]
        pltpu.make_async_copy(rest, rest, t_send.at[q]).wait()

    def landing(q, place):
        if q == 3 and place >= EARLY:
            return rb4.at[place - EARLY]
        return arrived[q].at[place]

    def gather(q, part):
        if part == 0:
            for s in range(SLOTS):
                arrived[q][0, s] = store[q][idxs[0, s]]
        for dy, dx in ORDER[part * 4:part * 4 + 4]:
            place = PLACE[dy, dx]
            asked = ((NY - dy) % NY) * NX + (NX - dx) % NX
            for s in range(SLOTS):
                outgoing[q][place, s] = store[q][idxs[asked, s]]
            pltpu.make_async_remote_copy(
                outgoing[q].at[place], landing(q, place),
                g_send.at[q], g_recv.at[q + 1 if q == 3 and place >= EARLY else q],
                device_id=partner(dy, dx), device_id_type=MESH,
            ).start()

    def gather_wait(q):
        if q == 4:
            rest = rb4
        else:
            rest = arrived[q].at[pl.ds(1, (EARLY if q == 3 else CHIPS) - 1)]
        pltpu.make_async_copy(rest, rest, g_recv.at[q]).wait()

    def stacked(t):
        rows = pl.ds(t * TILE, TILE)
        return jnp.concatenate([q_ref[rows, h * DIM:(h + 1) * DIM] for h in range(HEADS)], axis=0)

    def scores(a, b):
        return lax.dot_general(a, b, (((1,), (1,)), ((), ())), preferred_element_type=F32)

    def own(t):
        block, r = t // (BLOCK // TILE), t % (BLOCK // TILE)
        width = (r + 1) * TILE
        keys = k_ref[block].reshape(BLOCK, DIM)[:width]
        vals = v_ref[block].reshape(BLOCK, DIM)[:width]
        s = scores(stacked(t), keys)
        row = lax.broadcasted_iota(jnp.int32, s.shape, 0) % TILE + r * TILE
        col = lax.broadcasted_iota(jnp.int32, s.shape, 1)
        s = jnp.where(col <= row, s, -jnp.inf)
        m = jnp.max(s, axis=1, keepdims=True)
        p = jnp.exp2(s * SCALE2 - m * SCALE2)
        m_ref[t] = m
        l_ref[t] = jnp.sum(p, axis=1, keepdims=True)
        acc_ref[t] = jnp.dot(p.astype(BF16), vals, preferred_element_type=F32)

    def slot_of(t, e):
        entry = emap[t * 3 + e]
        return jnp.maximum(entry, 0), jnp.where(entry < 0, DEAD, 0.0).astype(F32)

    def remote_keys(t, carry):
        queries = stacked(t)
        m_own = m_ref[t]
        m = m_own
        parts = []
        for e in range(3):
            slot, bias = slot_of(t, e)
            keys = jnp.concatenate(
                [rb0[:, slot].reshape(KHALF, DIM), rb1[:, slot].reshape(KHALF, DIM)], axis=0)
            s = scores(queries, keys)
            m = jnp.maximum(m, jnp.max(s, axis=1, keepdims=True) + bias)
            parts.append((s, bias))
        m2 = m * SCALE2
        alpha = jnp.exp2(m_own * SCALE2 - m2)
        total = l_ref[t] * alpha
        for e, (s, bias) in enumerate(parts):
            p = jnp.exp2(s * SCALE2 - (m2 - bias))
            total = total + jnp.sum(p, axis=1, keepdims=True)
            p = p.astype(BF16)
            first = 0
            for p_ref, width in zip((p0_ref, p1_ref, p2_ref), WIDTHS):
                p_ref[t, :, e * width:(e + 1) * width] = p[:, first:first + width]
                first += width
        l_ref[t] = 1.0 / total
        acc_ref[t] = acc_ref[t] * alpha
        return carry

    def remote_values(stage):
        ref = (rb2, rb3, rb4)[stage]
        p_ref = (p0_ref, p1_ref, p2_ref)[stage]

        def one(t):
            slots = [slot_of(t, e)[0] for e in range(3)]
            vals = jnp.concatenate([ref[:, slot].reshape(WIDTHS[stage], DIM) for slot in slots], axis=0)
            acc = acc_ref[t] + jnp.dot(p_ref[t], vals, preferred_element_type=F32)
            if stage == 2:
                normed = (acc * l_ref[t]).astype(BF16)
                rows = pl.ds(pl.multiple_of(t * TILE, TILE), TILE)
                for h in range(HEADS):
                    out_ref[rows, h * DIM:(h + 1) * DIM] = normed[h * TILE:(h + 1) * TILE]
            else:
                acc_ref[t] = acc

        def step(pair, carry):
            one(pair * 2)
            one(pair * 2 + 1)
            return carry

        lax.fori_loop(0, TILES // 2, step, 0)

    spread(0)
    ask()
    spread(1)
    for i in range(PIECES):
        for way in range(2):
            ring_step(0, 0, LONG_FIRST[way][i], way)
    loads[2].wait()
    spread(2)
    spread(3)
    loads[3].wait()

    events = []
    for q in range(4):
        begin = 3.5 * q
        for i in range(PIECES):
            for way in range(2):
                for t in range(0 if q else 1, RING_STEPS + 1):
                    events.append((begin + t + i / PIECES, functools.partial(ring_step, q, t, LONG_FIRST[way][i], way)))
        events.append((begin + 4.3, functools.partial(across_wait, q)))
        for part in range(4):
            events.append((begin + 4.31 + 0.5 * part * (q < 3), functools.partial(gather, q, part)))
    for t in range(TILES):
        events.append((0.9 + OWN_EVERY * t, functools.partial(own, t)))
    events.append((KEYS_AT - 0.02, functools.partial(gather_wait, 0)))
    events.append((KEYS_AT - 0.01, functools.partial(gather_wait, 1)))
    for t in range(KEYS_EARLY):
        events.append((KEYS_AT + KEYS_EVERY * t, functools.partial(remote_keys, t, 0)))
    events.append((2.1, places))
    events.append((2.9, places_wait))
    for _, task in sorted(events, key=lambda event: event[0]):
        task()

    def key_pair(i, carry):
        remote_keys(KEYS_EARLY + 2 * i, 0)
        remote_keys(KEYS_EARLY + 2 * i + 1, 0)
        return carry

    lax.fori_loop(0, (TILES - KEYS_EARLY) // 2, key_pair, 0)
    rest = req.at[pl.ds(1, CHIPS - 1)]
    pltpu.make_async_copy(rest, rest, rq_send).wait()
    for q in range(4):
        ring_drain(q)
        if q < 3:
            rest = outgoing[q].at[pl.ds(1, CHIPS - 1)]
            pltpu.make_async_copy(rest, rest, g_send.at[q]).wait()
    gather_wait(2)
    remote_values(0)
    gather_wait(3)
    remote_values(1)
    gather_wait(4)
    remote_values(2)

    rest = outgoing[3].at[pl.ds(1, CHIPS - 1)]
    pltpu.make_async_copy(rest, rest, g_send.at[3]).wait()


def body(queries, keys, values, selected):
    tokens = keys.shape[0]
    view = (tokens // BLOCK, CHIPS, 2, 16, DIM)
    hbm = pl.BlockSpec(memory_space=pl.ANY)
    dma = pltpu.SemaphoreType.DMA
    scratch = (
        [
            pltpu.VMEM(queries.shape, BF16),
            pltpu.VMEM(view, BF16),
            pltpu.VMEM(view, BF16),
            pltpu.SMEM(selected.shape[::-1], jnp.int32),
        ]
        + [pltpu.VMEM((STORE, 16, DIM), BF16)] * 4
        + [pltpu.VMEM((CHIPS, SLOTS, 16, DIM), BF16)] * 7
        + [pltpu.VMEM((EARLY, SLOTS, 16, DIM), BF16), pltpu.VMEM((CHIPS - EARLY, SLOTS, 16, DIM), BF16)]
        + [
            pltpu.SMEM((ENTRIES,), jnp.int32),
            pltpu.VMEM((8, 128), jnp.int32),
            pltpu.VMEM((CHIPS, 8, 128), jnp.int32),
            pltpu.VMEM((CHIPS, 128), jnp.int32),
            pltpu.SMEM((CHIPS, 128), jnp.int32),
            *[pltpu.VMEM((TILES, HEADS * TILE, 3 * width), BF16) for width in WIDTHS],
            pltpu.VMEM((TILES, HEADS * TILE, 1), F32),
            pltpu.VMEM((TILES, HEADS * TILE, 1), F32),
            pltpu.VMEM((TILES, HEADS * TILE, DIM), F32),
            dma((4,)), dma, dma, dma,
            dma((4,)), dma((4, NY)),
            dma((4,)), dma((4, 2, RING_STEPS, PIECES)),
            dma((4,)),
            dma((4,)), dma((5,)),
        ]
    )
    return pl.pallas_call(
        kernel,
        out_shape=pltpu.VMEM(queries.shape, BF16),
        in_specs=[hbm] * 4,
        out_specs=pl.BlockSpec(memory_space=pltpu.VMEM),
        scratch_shapes=scratch,
        compiler_params=pltpu.CompilerParams(
            collective_id=0, has_side_effects=True, vmem_limit_bytes=56 << 20),
        cost_estimate=pl.CostEstimate(flops=4 << 30, bytes_accessed=8 << 20, transcendentals=8 << 20),
        name="moba",
    )(queries, keys.reshape(view), values.reshape(view), selected.T)


def solution(mesh):
    spec = P(("node", "local"), None)
    return jax.shard_map(
        body, mesh=mesh, in_specs=(spec,) * 4, out_specs=spec, check_vma=False)
```
